32 devices in a mesh: band: 4 (over y, x), gx: 4 (over z), gy: 2 (over core).
Axes of the slice: x: 2, y: 2, z: 4, core: 2. Of those that a mesh axis runs over, the one named last changes fastest.
Arguments:
- forward: bfloat16 [4, 2, 5, 4096, 1024], P('band', None, None, 'gx', 'gy'), may hold values from -6 to 6
- adjoint: bfloat16 [4, 2, 5, 4096, 1024], P('band', None, None, 'gx', 'gy'), may hold values from -6 to 6
- freq_index: int32 [4], P('band'), may hold values from 0 to 15
- span_index: int32 [4], P('band'), may hold values from 0 to 15
Outputs:
- sensitivity: float32 [5, 4096, 1024], P(None, ('gx', 'band'), 'gy')
The draws below stay inside these ranges and needn't reach their ends.
All inputs are finite; a program needn't handle non-finite values.
Results may differ from the reference program's by a relative error of at most 0.0003.
Values may be sent and summed in bfloat16 or wider, within the bound.
A program may use at most 128 MiB of HBM per device.

```python
import math
import jax
import jax.numpy as jnp
from jax import lax

COMPS = 5
FREQS = 16
SPANS = 16
OUTS = 5
MODES = 4
NX = 4096
NY = 1024


def plant(drawn, stream_key, smallest, high):
    longest = drawn.shape.index(max(drawn.shape))
    spots = []
    for shift in (0, 1):
        where = [jax.random.randint(jax.random.fold_in(stream_key, axis), (), 0, length) for axis, length in enumerate(drawn.shape)]
        where[longest] = (where[longest] + shift) % drawn.shape[longest]
        spots.append(tuple(where))
    return drawn.at[spots[0]].set(smallest).at[spots[1]].set(high)


def levels(rng, dims, pieces, least, top_value):
    loudness = 1.0
    for position, shards_of in pieces:
        heights = jax.random.uniform(jax.random.fold_in(jax.random.fold_in(rng, 6), position), (shards_of,), jnp.float32, least / len(pieces), top_value / len(pieces))
        loudness = loudness * jnp.repeat(jnp.exp(heights), dims[position] // shards_of).reshape((-1,) + (1,) * (len(dims) - 1 - position))
    return loudness


def normal_values(own_key, dims, scale, most, shards=(), kind=jnp.bfloat16):
    loudness = levels(own_key, dims, shards, -0.22, 0.18) if shards else 1.0
    array = jax.random.normal(own_key, dims, jnp.float32) * scale * loudness
    return jnp.minimum(jnp.maximum(array, -most), most).astype(kind)


def setup_inputs(seed: int = 0) -> dict:
    key_of = jax.random.split(jax.random.key(seed), 5)
    forward = normal_values(key_of[0], (MODES, 2, COMPS, NX, NY), 1.0, 6.0, ((0, 4), (3, 4), (4, 2)))
    adjoint = normal_values(key_of[1], (MODES, 2, COMPS, NX, NY), 1.0, 6.0, ((0, 4), (3, 4), (4, 2)))
    freq_index = plant(jax.random.randint(key_of[2], (MODES,), 0, FREQS), jax.random.fold_in(key_of[2], 1), 0, FREQS - 1).astype(jnp.int32)
    span_index = plant(jax.random.randint(key_of[3], (MODES,), 0, SPANS), jax.random.fold_in(key_of[3], 1), 0, SPANS - 1).astype(jnp.int32)
    return {"forward": forward, "adjoint": adjoint, "freq_index": freq_index, "span_index": span_index}


def central(field, axis):
    pad_width = [(0, 0)] * field.ndim
    pad_width[axis] = (2, 2)
    padded = jnp.pad(field, pad_width)
    count = field.shape[axis]

    def offset_part(offset):
        return lax.slice_in_dim(padded, offset, offset + count, axis=axis)
    return (8.0 * (offset_part(3) - offset_part(1)) - (offset_part(4) - offset_part(0))) / 12.0

def reference(forward, adjoint, freq_index, span_index):
    omega = (freq_index.astype(jnp.float32) + 1.0) / FREQS
    beta = (span_index.astype(jnp.float32) - (SPANS - 1) / 2.0) * 2.0 / SPANS
    weight = 1.0 / (0.5 + omega)

    def add_mode(total, items):
        forward_mode, adjoint_mode, omega_m, beta_m, weight_m = items
        shape_q = forward_mode.astype(jnp.float32)
        shape_a = adjoint_mode.astype(jnp.float32)
        along_x = central(shape_q, 2)
        along_y = central(shape_q, 3)
        gradient_x = lax.optimization_barrier(jnp.sum(shape_a[0] * along_x[0] + shape_a[1] * along_x[1], axis=0))
        gradient_y = lax.optimization_barrier(jnp.sum(shape_a[0] * along_y[0] + shape_a[1] * along_y[1], axis=0))
        cross = lax.optimization_barrier(jnp.sum(shape_a[0] * shape_q[1] - shape_a[1] * shape_q[0], axis=0))
        direct = lax.optimization_barrier(jnp.sum(shape_a[0] * shape_q[0] + shape_a[1] * shape_q[1], axis=0))
        stacked = jnp.stack([gradient_x, gradient_y, -beta_m * cross, omega_m * cross, direct])
        return (total + weight_m * stacked, None)
    start = jnp.zeros((OUTS, forward.shape[3], forward.shape[4]), jnp.float32)
    total, unused = lax.scan(add_mode, start, (forward, adjoint, omega, beta, weight))
    return total * (1.0 / math.sqrt(5.0 * MODES))
```

```python
import functools
import math

import jax
import jax.numpy as jnp
from jax import lax
from jax.experimental import pallas as pl
from jax.experimental.pallas import tpu as pltpu
from jax.sharding import PartitionSpec as P

FREQS = 16
SPANS = 16
ROWS = 128
SIDE = 16
LANES = 128
SLOTS = 3
LEVELS = 32767.0


def band_matrix(shape, offset, row_minus_column):
    row = lax.broadcasted_iota(jnp.int32, shape, 0)
    column = lax.broadcasted_iota(jnp.int32, shape, 1)
    d = (row - column if row_minus_column else column - row) - offset
    value = jnp.where(d == 1, 8.0, 0.0)
    value = jnp.where(d == -1, -8.0, value)
    value = jnp.where(d == 2, -1.0, value)
    value = jnp.where(d == -2, 1.0, value)
    return value.astype(jnp.bfloat16)


def kernel(
    bands, gxs, comps, pieces, modes,
    freq_ref, span_ref, fwd_ref, adj_ref, out_ref,
    ext, adj, acc, along_a, along_b, sent, sent_scale, got, got_scale, total, coef,
    fwd_sem, adj_sem, x_send, x_recv, y_send, y_recv,
    d_send, d_recv, s_send, s_recv, out_sem,
):
    band = lax.axis_index("band")
    gx = lax.axis_index("gx")
    gy = lax.axis_index("gy")
    nx, ny = fwd_ref.shape[1], fwd_ref.shape[2]
    others = bands - 1
    remote = others * pieces
    steps = bands * pieces
    half = 256

    def peer(k):
        if bands == 4:
            high = (band // 2 + k // 2) % 2
            return high * 2 + (band % 2 + k % 2) % 2
        return (band + k) % bands

    def place(t):
        own = t // remote
        k = (1 - own) * (others - t % others)
        piece = (1 - own) * (t // others) + own * (t - remote)
        return k, piece

    def row_of(t):
        k, piece = place(t)
        return pl.multiple_of((peer(k) * pieces + piece) * ROWS, ROWS)

    def adj_copy(t):
        slot = t % SLOTS
        return pltpu.make_async_copy(
            adj_ref.at[:, pl.ds(row_of(t), ROWS), :], adj.at[slot], adj_sem.at[slot]
        )

    fwd_copy = pltpu.make_async_copy(
        fwd_ref, ext.at[:, pl.ds(SIDE, nx), pl.ds(LANES, ny)], fwd_sem
    )
    fwd_copy.start()
    for t in range(SLOTS):
        adj_copy(t).start()

    barrier = pltpu.get_barrier_semaphore()
    for k in range(1, bands):
        target = peer(k)
        pl.semaphore_signal(barrier, inc=1, device_id={"band": target})
    pl.semaphore_signal(barrier, inc=1, device_id={"gy": 1 - gy})

    @pl.when(gx > 0)
    def _():
        pl.semaphore_signal(barrier, inc=1, device_id={"gx": gx - 1})

    @pl.when(gx < gxs - 1)
    def _():
        pl.semaphore_signal(barrier, inc=1, device_id={"gx": gx + 1})

    along_a[...] = band_matrix((ROWS, ROWS + 2 * SIDE), SIDE, False)
    along_b[...] = band_matrix((half + 2 * LANES, half), LANES, True)
    freq = jnp.full((1, ny), freq_ref[0], jnp.int32).astype(jnp.float32)
    span = jnp.full((1, ny), span_ref[0], jnp.int32).astype(jnp.float32)
    omega = (freq + 1.0) / FREQS
    beta = (span - (SPANS - 1) / 2.0) * 2.0 / SPANS
    weight = (1.0 / math.sqrt(comps * modes)) / (0.5 + omega)
    coef[0:1] = weight / 12.0
    coef[1:2] = weight / 12.0
    coef[2:3] = -beta * weight
    coef[3:4] = omega * weight
    coef[4:5] = weight

    @pl.when(gx == 0)
    def _():
        ext[:, 0:SIDE, LANES:LANES + ny] = jnp.zeros((2 * comps, SIDE, ny), jnp.bfloat16)

    @pl.when(gx == gxs - 1)
    def _():
        ext[:, SIDE + nx:, LANES:LANES + ny] = jnp.zeros((2 * comps, SIDE, ny), jnp.bfloat16)

    @pl.when(gy == 0)
    def _():
        for p in range(2 * comps):
            ext[p, SIDE:SIDE + nx, 0:LANES] = jnp.zeros((nx, LANES), jnp.bfloat16)

    @pl.when(gy == 1)
    def _():
        for p in range(2 * comps):
            ext[p, SIDE:SIDE + nx, LANES + ny:] = jnp.zeros((nx, LANES), jnp.bfloat16)

    below = (gx + gxs - 1) // gxs
    above = (2 * gxs - 2 - gx) // gxs
    pl.semaphore_wait(barrier, bands + below + above)

    def x_copy(up):
        source = nx - SIDE if up else 0
        target = 0 if up else SIDE + nx
        return pltpu.make_async_remote_copy(
            fwd_ref.at[:, pl.ds(source, SIDE), :],
            ext.at[:, pl.ds(target, SIDE), pl.ds(LANES, ny)],
            x_send.at[int(up)],
            x_recv.at[int(up)],
            device_id={"gx": gx + 1 if up else gx - 1},
        )

    def y_copy(t):
        rows = row_of(t)
        source = pl.multiple_of((1 - gy) * (ny - LANES), LANES)
        target = pl.multiple_of(gy * (LANES + ny), LANES)
        return pltpu.make_async_remote_copy(
            fwd_ref.at[:, pl.ds(rows, ROWS), pl.ds(source, LANES)],
            ext.at[:, pl.ds(rows + SIDE, ROWS), pl.ds(target, LANES)],
            y_send.at[t],
            y_recv.at[t],
            device_id={"gy": 1 - gy},
        )

    @pl.when(gx < gxs - 1)
    def _():
        x_copy(True).start()

    @pl.when(gx > 0)
    def _():
        x_copy(False).start()

    def start_y(t, carry):
        y_copy(t).start()
        return carry

    lax.fori_loop(0, steps, start_y, 0)
    fwd_copy.wait()

    @pl.when(gx > 0)
    def _():
        x_copy(True).wait_recv()

    @pl.when(gx < gxs - 1)
    def _():
        x_copy(False).wait_recv()

    def data_copy(k, piece):
        return pltpu.make_async_remote_copy(
            sent.at[k - 1, piece], got.at[k - 1, piece],
            d_send.at[k - 1, piece], d_recv.at[k - 1, piece],
            device_id={"band": peer(k)},
        )

    def scale_copy(k, piece):
        return pltpu.make_async_remote_copy(
            sent_scale.at[k - 1, piece], got_scale.at[k - 1, piece],
            s_send.at[k - 1, piece], s_recv.at[k - 1, piece],
            device_id={"band": peer(k)},
        )

    def step(t, carry):
        k, piece = place(t)
        rows = row_of(t)
        slot = t % SLOTS
        adj_copy(t).wait()
        y_copy(t).wait_recv()
        acc[...] = jnp.zeros_like(acc)

        def add_comp(comp, carry):
            for h in range(ny // half):
                cols = pl.ds(h * half, half)
                dx, dy, q, a = [], [], [], []
                for part in range(2):
                    plane = part * comps + comp
                    tall = ext[plane, pl.ds(rows, ROWS + 2 * SIDE), pl.ds(LANES + h * half, half)]
                    wide = ext[plane, pl.ds(rows + SIDE, ROWS), pl.ds(h * half, half + 2 * LANES)]
                    dx.append(jnp.dot(along_a[...], tall, preferred_element_type=jnp.float32))
                    dy.append(jnp.dot(wide, along_b[...], preferred_element_type=jnp.float32))
                    q.append(wide[:, LANES:LANES + half].astype(jnp.float32))
                    a.append(adj[slot, plane, :, cols].astype(jnp.float32))
                acc[0, :, cols] += a[0] * dx[0] + a[1] * dx[1]
                acc[1, :, cols] += a[0] * dy[0] + a[1] * dy[1]
                acc[2, :, cols] += a[0] * q[1] - a[1] * q[0]
                acc[3, :, cols] += a[0] * q[0] + a[1] * q[1]
            return carry

        lax.fori_loop(0, comps, add_comp, 0)

        @pl.when(t + SLOTS < steps)
        def _():
            adj_copy(t + SLOTS).start()

        @pl.when(t < remote)
        def _():
            for field in range(4):
                value = acc[field]
                most = jnp.maximum(jnp.max(jnp.abs(value), axis=0, keepdims=True), 1e-30)
                level = jnp.round(value * (LEVELS / most))
                sent[k - 1, piece, field] = level.astype(jnp.int32).astype(jnp.int16)
                scale = most * (1.0 / LEVELS)
                if field < 3:
                    sent_scale[k - 1, piece, field:field + 1] = scale * coef[field:field + 1]
                if field >= 2:
                    sent_scale[k - 1, piece, field + 1:field + 2] = scale * coef[field + 1:field + 2]
            data_copy(k, piece).start()
            scale_copy(k, piece).start()

        @pl.when(t >= remote)
        def _():
            for out, field in enumerate((0, 1, 2, 2, 3)):
                total[out, pl.ds(pl.multiple_of(piece * ROWS, ROWS), ROWS), :] = (
                    acc[field] * coef[out:out + 1]
                )

        return carry

    sent_scale[...] = jnp.zeros_like(sent_scale)
    lax.fori_loop(0, steps, step, 0)

    def out_copy(piece):
        rows = pl.ds(pl.multiple_of(piece * ROWS, ROWS), ROWS)
        return pltpu.make_async_copy(
            total.at[:, rows, :], out_ref.at[:, rows, :], out_sem.at[piece]
        )

    def gather(t, carry):
        k, piece = place(t)
        data_copy(k, piece).wait_recv()
        scale_copy(k, piece).wait_recv()
        rows = pl.ds(pl.multiple_of(piece * ROWS, ROWS), ROWS)
        for field in range(4):
            value = got[k - 1, piece, field].astype(jnp.int32).astype(jnp.float32)
            if field < 3:
                total[field, rows, :] += value * got_scale[k - 1, piece, field:field + 1]
            if field >= 2:
                total[field + 1, rows, :] += value * got_scale[k - 1, piece, field + 1:field + 2]

        @pl.when(t % others == others - 1)
        def _():
            out_copy(piece).start()

        return carry

    lax.fori_loop(0, remote, gather, 0)

    def finish(t, carry):
        k, piece = place(t)
        data_copy(k, piece).wait_send()
        scale_copy(k, piece).wait_send()
        return carry

    lax.fori_loop(0, remote, finish, 0)

    def finish_y(t, carry):
        y_copy(t).wait_send()
        return carry

    lax.fori_loop(0, steps, finish_y, 0)

    @pl.when(gx < gxs - 1)
    def _():
        x_copy(True).wait_send()

    @pl.when(gx > 0)
    def _():
        x_copy(False).wait_send()

    def finish_out(piece, carry):
        out_copy(piece).wait()
        return carry

    lax.fori_loop(0, pieces, finish_out, 0)


def local(bands, gxs, forward, adjoint, freq_index, span_index):
    comps, nx, ny = forward.shape[2:]
    pieces = nx // bands // ROWS
    steps = bands * pieces
    others = bands - 1
    planes = 2 * comps
    anywhere = pl.BlockSpec(memory_space=pl.ANY)
    scalar = pl.BlockSpec(memory_space=pltpu.SMEM)
    dma = pltpu.SemaphoreType.DMA
    return pl.pallas_call(
        functools.partial(kernel, bands, gxs, comps, pieces, forward.shape[0] * bands),
        out_shape=jax.ShapeDtypeStruct((5, nx // bands, ny), jnp.float32),
        in_specs=[scalar, scalar, anywhere, anywhere],
        out_specs=anywhere,
        scratch_shapes=[
            pltpu.VMEM((planes, nx + 2 * SIDE, ny + 2 * LANES), jnp.bfloat16),
            pltpu.VMEM((SLOTS, planes, ROWS, ny), jnp.bfloat16),
            pltpu.VMEM((4, ROWS, ny), jnp.float32),
            pltpu.VMEM((ROWS, ROWS + 2 * SIDE), jnp.bfloat16),
            pltpu.VMEM((256 + 2 * LANES, 256), jnp.bfloat16),
            pltpu.VMEM((others, pieces, 4, ROWS, ny), jnp.int16),
            pltpu.VMEM((others, pieces, 8, ny), jnp.float32),
            pltpu.VMEM((others, pieces, 4, ROWS, ny), jnp.int16),
            pltpu.VMEM((others, pieces, 8, ny), jnp.float32),
            pltpu.VMEM((5, nx // bands, ny), jnp.float32),
            pltpu.VMEM((8, ny), jnp.float32),
            dma(()), dma((SLOTS,)), dma((2,)), dma((2,)), dma((steps,)), dma((steps,)),
            dma((others, pieces)), dma((others, pieces)),
            dma((others, pieces)), dma((others, pieces)), dma((pieces,)),
        ],
        compiler_params=pltpu.CompilerParams(
            collective_id=0, has_side_effects=True, vmem_limit_bytes=60 * 1024 * 1024
        ),
        cost_estimate=pl.CostEstimate(
            flops=20 * planes * nx * ny, bytes_accessed=4 * planes * nx * ny, transcendentals=0
        ),
    )(
        freq_index, span_index,
        forward.reshape(planes, nx, ny), adjoint.reshape(planes, nx, ny),
    )


def solution(mesh):
    in_specs = (
        P("band", None, None, "gx", "gy"),
        P("band", None, None, "gx", "gy"),
        P("band"),
        P("band"),
    )
    out_specs = P(None, ("gx", "band"), "gy")
    body = functools.partial(local, mesh.shape["band"], mesh.shape["gx"])
    return jax.shard_map(body, mesh=mesh, in_specs=in_specs, out_specs=out_specs, check_vma=False)
```

```python
import functools
import math

import jax
import jax.numpy as jnp
from jax import lax
from jax.experimental import pallas as pl
from jax.experimental.pallas import tpu as pltpu
from jax.sharding import PartitionSpec as P

FREQS = 16
SPANS = 16
ROWS = 128
SIDE = 16
LANES = 128
SLOTS = 3
LEVELS = 32767.0


def band_matrix(shape, offset, row_minus_column):
    row = lax.broadcasted_iota(jnp.int32, shape, 0)
    column = lax.broadcasted_iota(jnp.int32, shape, 1)
    d = (row - column if row_minus_column else column - row) - offset
    value = jnp.where(d == 1, 8.0, 0.0)
    value = jnp.where(d == -1, -8.0, value)
    value = jnp.where(d == 2, -1.0, value)
    value = jnp.where(d == -2, 1.0, value)
    return value.astype(jnp.bfloat16)


def kernel(
    bands, gxs, comps, pieces, modes,
    freq_ref, span_ref, fwd_ref, adj_ref, out_ref,
    ext, adj, acc, along_a, along_b, sent, sent_sum, sent_scale,
    got, got_sum, got_scale, total, coef,
    joint_sem, strip_sem, adj_sem, x_send, x_recv, y_send, y_recv,
    d_send, d_recv, s_send, s_recv, out_sem,
):
    band = lax.axis_index("band")
    gx = lax.axis_index("gx")
    gy = lax.axis_index("gy")
    nx, ny = fwd_ref.shape[1], fwd_ref.shape[2]
    steps = bands * pieces
    quarter = nx // bands
    half = 256

    def peer(k):
        high = (band // 2 + k // 2) % 2
        return high * 2 + (band % 2 + k % 2) % 2

    def place(t):
        phase, piece = t // pieces, t % pieces
        odd = piece % 2
        last = phase // 3
        third = phase // 2 - last
        first = (3 - phase) // 3
        second = 1 - first - third - last
        return 3 * first + (1 + odd) * second + (2 - odd) * third, piece

    def row_of(t):
        k, piece = place(t)
        return pl.multiple_of((peer(k) * pieces + piece) * ROWS, ROWS)

    def adj_copy(t):
        slot = t % SLOTS
        return pltpu.make_async_copy(
            adj_ref.at[:, pl.ds(row_of(t), ROWS), :], adj.at[slot], adj_sem.at[slot]
        )

    def joint_copy(edge):
        low, high = max(edge * quarter - SIDE, 0), min(edge * quarter + SIDE, nx)
        return pltpu.make_async_copy(
            fwd_ref.at[:, pl.ds(low, high - low), :],
            ext.at[:, pl.ds(SIDE + low, high - low), pl.ds(LANES, ny)],
            joint_sem.at[edge],
        )

    def strip_copy(k):
        low = pl.multiple_of(peer(k) * quarter + SIDE, SIDE)
        rows = quarter - 2 * SIDE
        return pltpu.make_async_copy(
            fwd_ref.at[:, pl.ds(low, rows), :],
            ext.at[:, pl.ds(low + SIDE, rows), pl.ds(LANES, ny)],
            strip_sem.at[k],
        )

    for edge in range(bands + 1):
        joint_copy(edge).start()
    strip_copy(3).start()
    adj_copy(0).start()

    barrier = pltpu.get_barrier_semaphore()
    for k in range(1, bands):
        target = peer(k)
        pl.semaphore_signal(barrier, inc=1, device_id={"band": target})
    pl.semaphore_signal(barrier, inc=1, device_id={"gy": 1 - gy})

    @pl.when(gx > 0)
    def _():
        pl.semaphore_signal(barrier, inc=1, device_id={"gx": gx - 1})

    @pl.when(gx < gxs - 1)
    def _():
        pl.semaphore_signal(barrier, inc=1, device_id={"gx": gx + 1})

    along_a[...] = band_matrix((ROWS, ROWS + 2 * SIDE), SIDE, False)
    along_b[...] = band_matrix((half + 2 * LANES, half), LANES, True)
    freq = jnp.full((1, ny), freq_ref[0], jnp.int32).astype(jnp.float32)
    span = jnp.full((1, ny), span_ref[0], jnp.int32).astype(jnp.float32)
    omega = (freq + 1.0) / FREQS
    beta = (span - (SPANS - 1) / 2.0) * 2.0 / SPANS
    weight = (1.0 / math.sqrt(comps * modes)) / (0.5 + omega)
    coef[0:1] = weight / 12.0
    coef[1:2] = weight / 12.0
    coef[2:3] = -beta * weight
    coef[3:4] = omega * weight
    coef[4:5] = weight

    @pl.when(gx == 0)
    def _():
        ext[:, 0:SIDE, LANES:LANES + ny] = jnp.zeros((2 * comps, SIDE, ny), jnp.bfloat16)

    @pl.when(gx == gxs - 1)
    def _():
        ext[:, SIDE + nx:, LANES:LANES + ny] = jnp.zeros((2 * comps, SIDE, ny), jnp.bfloat16)

    @pl.when(gy == 0)
    def _():
        for p in range(2 * comps):
            ext[p, SIDE:SIDE + nx, 0:LANES] = jnp.zeros((nx, LANES), jnp.bfloat16)

    @pl.when(gy == 1)
    def _():
        for p in range(2 * comps):
            ext[p, SIDE:SIDE + nx, LANES + ny:] = jnp.zeros((nx, LANES), jnp.bfloat16)

    below = (gx + gxs - 1) // gxs
    above = (2 * gxs - 2 - gx) // gxs
    pl.semaphore_wait(barrier, bands + below + above)

    def x_copy(up):
        source = nx - SIDE if up else 0
        target = 0 if up else SIDE + nx
        return pltpu.make_async_remote_copy(
            fwd_ref.at[:, pl.ds(source, SIDE), :],
            ext.at[:, pl.ds(target, SIDE), pl.ds(LANES, ny)],
            x_send.at[int(up)],
            x_recv.at[int(up)],
            device_id={"gx": gx + 1 if up else gx - 1},
        )

    def y_copy(t):
        rows = row_of(t)
        source = pl.multiple_of((1 - gy) * (ny - LANES), LANES)
        target = pl.multiple_of(gy * (LANES + ny), LANES)
        return pltpu.make_async_remote_copy(
            fwd_ref.at[:, pl.ds(rows, ROWS), pl.ds(source, LANES)],
            ext.at[:, pl.ds(rows + SIDE, ROWS), pl.ds(target, LANES)],
            y_send.at[t],
            y_recv.at[t],
            device_id={"gy": 1 - gy},
        )

    @pl.when(gx < gxs - 1)
    def _():
        x_copy(True).start()

    @pl.when(gx > 0)
    def _():
        x_copy(False).start()

    def start_y(t, carry):
        y_copy(t).start()
        return carry

    lax.fori_loop(0, pieces, start_y, 0)
    for edge in range(bands + 1):
        joint_copy(edge).wait()
    strip_copy(3).wait()
    for t in range(1, SLOTS):
        adj_copy(t).start()
    for k in (1, 2, 0):
        strip_copy(k).start()
    lax.fori_loop(pieces, steps, start_y, 0)

    @pl.when(gx > 0)
    def _():
        x_copy(True).wait_recv()

    @pl.when(gx < gxs - 1)
    def _():
        x_copy(False).wait_recv()

    def data_copy(phase, piece):
        return pltpu.make_async_remote_copy(
            sent.at[phase, piece], got.at[phase, piece],
            d_send.at[phase, piece], d_recv.at[phase, piece],
            device_id={"band": peer(1 + piece % 2)},
        )

    def sum_copy(piece):
        return pltpu.make_async_remote_copy(
            sent_sum.at[piece], got_sum.at[piece],
            d_send.at[2, piece], d_recv.at[2, piece],
            device_id={"band": peer(2 - piece % 2)},
        )

    def scale_copy(phase, piece):
        odd = piece % 2
        third = phase // 2
        return pltpu.make_async_remote_copy(
            sent_scale.at[phase, piece], got_scale.at[phase, piece],
            s_send.at[phase, piece], s_recv.at[phase, piece],
            device_id={"band": peer((1 + odd) * (1 - third) + (2 - odd) * third)},
        )

    fields = (0, 1, 2, 2, 3)

    def coded(value):
        most = jnp.maximum(jnp.max(jnp.abs(value), axis=0, keepdims=True), 1e-30)
        level = jnp.round(value * (LEVELS / most))
        return level.astype(jnp.int32).astype(jnp.int16), most * (1.0 / LEVELS)

    def step(t, carry):
        phase, piece = t // pieces, t % pieces
        rows = row_of(t)
        slot = t % SLOTS

        @pl.when(t == pieces)
        def _():
            strip_copy(1).wait()
            strip_copy(2).wait()

        @pl.when(t == 3 * pieces)
        def _():
            strip_copy(0).wait()

        adj_copy(t).wait()
        y_copy(t).wait_recv()
        acc[...] = jnp.zeros_like(acc)

        def add_comp(comp, carry):
            for h in range(ny // half):
                cols = pl.ds(h * half, half)
                dx, dy, q, a = [], [], [], []
                for part in range(2):
                    plane = part * comps + comp
                    tall = ext[plane, pl.ds(rows, ROWS + 2 * SIDE), pl.ds(LANES + h * half, half)]
                    wide = ext[plane, pl.ds(rows + SIDE, ROWS), pl.ds(h * half, half + 2 * LANES)]
                    dx.append(jnp.dot(along_a[...], tall, preferred_element_type=jnp.float32))
                    dy.append(jnp.dot(wide, along_b[...], preferred_element_type=jnp.float32))
                    q.append(wide[:, LANES:LANES + half].astype(jnp.float32))
                    a.append(adj[slot, plane, :, cols].astype(jnp.float32))
                acc[0, :, cols] += a[0] * dx[0] + a[1] * dx[1]
                acc[1, :, cols] += a[0] * dy[0] + a[1] * dy[1]
                acc[2, :, cols] += a[0] * q[1] - a[1] * q[0]
                acc[3, :, cols] += a[0] * q[0] + a[1] * q[1]
            return carry

        lax.fori_loop(0, comps, add_comp, 0)

        @pl.when(t + SLOTS < steps)
        def _():
            adj_copy(t + SLOTS).start()

        @pl.when(phase < 2)
        def _():
            for field in range(4):
                level, scale = coded(acc[field])
                sent[phase, piece, field] = level
                for out in range(5):
                    if fields[out] == field:
                        sent_scale[phase, piece, out:out + 1] = scale * coef[out:out + 1]
            data_copy(phase, piece).start()
            scale_copy(phase, piece).start()

        @pl.when(phase == 2)
        def _():
            data_copy(0, piece).wait_recv()
            scale_copy(0, piece).wait_recv()
            for out, field in enumerate(fields):
                other = got[0, piece, field].astype(jnp.int32).astype(jnp.float32)
                value = acc[field] * coef[out:out + 1] + other * got_scale[0, piece, out:out + 1]
                level, scale = coded(value)
                sent_sum[piece, out] = level
                sent_scale[2, piece, out:out + 1] = scale
            sum_copy(piece).start()
            scale_copy(2, piece).start()

        @pl.when(phase == 3)
        def _():
            for out, field in enumerate(fields):
                total[out, pl.ds(pl.multiple_of(piece * ROWS, ROWS), ROWS), :] = (
                    acc[field] * coef[out:out + 1]
                )

        return carry

    sent_scale[...] = jnp.zeros_like(sent_scale)
    lax.fori_loop(0, steps, step, 0)

    def out_copy(piece):
        rows = pl.ds(pl.multiple_of(piece * ROWS, ROWS), ROWS)
        return pltpu.make_async_copy(
            total.at[:, rows, :], out_ref.at[:, rows, :], out_sem.at[piece]
        )

    def add_one(piece, carry):
        data_copy(1, piece).wait_recv()
        scale_copy(1, piece).wait_recv()
        rows = pl.ds(pl.multiple_of(piece * ROWS, ROWS), ROWS)
        for out, field in enumerate(fields):
            value = got[1, piece, field].astype(jnp.int32).astype(jnp.float32)
            total[out, rows, :] += value * got_scale[1, piece, out:out + 1]
        return carry

    lax.fori_loop(0, pieces, add_one, 0)

    def add_sum(piece, carry):
        sum_copy(piece).wait_recv()
        scale_copy(2, piece).wait_recv()
        rows = pl.ds(pl.multiple_of(piece * ROWS, ROWS), ROWS)
        for out in range(5):
            value = got_sum[piece, out].astype(jnp.int32).astype(jnp.float32)
            total[out, rows, :] += value * got_scale[2, piece, out:out + 1]
        out_copy(piece).start()
        return carry

    lax.fori_loop(0, pieces, add_sum, 0)

    def finish(piece, carry):
        for phase in range(2):
            data_copy(phase, piece).wait_send()
        sum_copy(piece).wait_send()
        for phase in range(3):
            scale_copy(phase, piece).wait_send()
        return carry

    lax.fori_loop(0, pieces, finish, 0)

    def finish_y(t, carry):
        y_copy(t).wait_send()
        return carry

    lax.fori_loop(0, steps, finish_y, 0)

    @pl.when(gx < gxs - 1)
    def _():
        x_copy(True).wait_send()

    @pl.when(gx > 0)
    def _():
        x_copy(False).wait_send()

    def finish_out(piece, carry):
        out_copy(piece).wait()
        return carry

    lax.fori_loop(0, pieces, finish_out, 0)


def local(bands, gxs, forward, adjoint, freq_index, span_index):
    comps, nx, ny = forward.shape[2:]
    pieces = nx // bands // ROWS
    steps = bands * pieces
    planes = 2 * comps
    anywhere = pl.BlockSpec(memory_space=pl.ANY)
    scalar = pl.BlockSpec(memory_space=pltpu.SMEM)
    dma = pltpu.SemaphoreType.DMA
    return pl.pallas_call(
        functools.partial(kernel, bands, gxs, comps, pieces, forward.shape[0] * bands),
        out_shape=jax.ShapeDtypeStruct((5, nx // bands, ny), jnp.float32),
        in_specs=[scalar, scalar, anywhere, anywhere],
        out_specs=anywhere,
        scratch_shapes=[
            pltpu.VMEM((planes, nx + 2 * SIDE, ny + 2 * LANES), jnp.bfloat16),
            pltpu.VMEM((SLOTS, planes, ROWS, ny), jnp.bfloat16),
            pltpu.VMEM((4, ROWS, ny), jnp.float32),
            pltpu.VMEM((ROWS, ROWS + 2 * SIDE), jnp.bfloat16),
            pltpu.VMEM((256 + 2 * LANES, 256), jnp.bfloat16),
            pltpu.VMEM((2, pieces, 4, ROWS, ny), jnp.int16),
            pltpu.VMEM((pieces, 5, ROWS, ny), jnp.int16),
            pltpu.VMEM((3, pieces, 8, ny), jnp.float32),
            pltpu.VMEM((2, pieces, 4, ROWS, ny), jnp.int16),
            pltpu.VMEM((pieces, 5, ROWS, ny), jnp.int16),
            pltpu.VMEM((3, pieces, 8, ny), jnp.float32),
            pltpu.VMEM((5, nx // bands, ny), jnp.float32),
            pltpu.VMEM((8, ny), jnp.float32),
            dma((bands + 1,)), dma((bands,)), dma((SLOTS,)), dma((2,)), dma((2,)), dma((steps,)), dma((steps,)),
            dma((3, pieces)), dma((3, pieces)),
            dma((3, pieces)), dma((3, pieces)), dma((pieces,)),
        ],
        compiler_params=pltpu.CompilerParams(
            collective_id=0, has_side_effects=True, vmem_limit_bytes=60 * 1024 * 1024
        ),
        cost_estimate=pl.CostEstimate(
            flops=20 * planes * nx * ny, bytes_accessed=4 * planes * nx * ny, transcendentals=0
        ),
    )(
        freq_index, span_index,
        forward.reshape(planes, nx, ny), adjoint.reshape(planes, nx, ny),
    )


def solution(mesh):
    in_specs = (
        P("band", None, None, "gx", "gy"),
        P("band", None, None, "gx", "gy"),
        P("band"),
        P("band"),
    )
    out_specs = P(None, ("gx", "band"), "gy")
    body = functools.partial(local, mesh.shape["band"], mesh.shape["gx"])
    return jax.shard_map(body, mesh=mesh, in_specs=in_specs, out_specs=out_specs, check_vma=False)
```

```python
import functools
import math

import jax
import jax.numpy as jnp
from jax import lax
from jax.experimental import pallas as pl
from jax.experimental.pallas import tpu as pltpu
from jax.sharding import PartitionSpec as P

FREQS = 16
SPANS = 16
ROWS = 128
SIDE = 16
LANES = 128
SLOTS = 3
LEVELS = 32767.0


def band_matrix(shape, offset, row_minus_column):
    row = lax.broadcasted_iota(jnp.int32, shape, 0)
    column = lax.broadcasted_iota(jnp.int32, shape, 1)
    d = (row - column if row_minus_column else column - row) - offset
    value = jnp.where(d == 1, 8.0, 0.0)
    value = jnp.where(d == -1, -8.0, value)
    value = jnp.where(d == 2, -1.0, value)
    value = jnp.where(d == -2, 1.0, value)
    return value.astype(jnp.bfloat16)


def kernel(
    bands, gxs, comps, pieces,
    freq_ref, span_ref, fwd_ref, adj_ref, out_ref,
    ext, adj, acc, along_a, along_b, sent, sent_sum, sent_scale,
    got, got_sum, got_scale, total, coef,
    joint_sem, strip_sem, adj_sem, x_send, x_recv, y_send, y_recv,
    d_send, d_recv, s_send, s_recv, out_sem,
):
    band = lax.axis_index("band")
    gx = lax.axis_index("gx")
    gy = lax.axis_index("gy")
    nx, ny = fwd_ref.shape[1], fwd_ref.shape[2]
    steps = bands * pieces
    quarter = nx // bands
    half = 256

    def peer(k):
        high = (band // 2 + k // 2) % 2
        return high * 2 + (band % 2 + k % 2) % 2

    def place(t):
        phase, piece = t // pieces, t % pieces
        odd = piece % 2
        last = phase // 3
        third = phase // 2 - last
        first = (3 - phase) // 3
        second = 1 - first - third - last
        return 3 * first + (1 + odd) * second + (2 - odd) * third, piece

    def row_of(t):
        k, piece = place(t)
        return pl.multiple_of((peer(k) * pieces + piece) * ROWS, ROWS)

    def adj_copy(t):
        slot = t % SLOTS
        return pltpu.make_async_copy(
            adj_ref.at[:, pl.ds(row_of(t), ROWS), :], adj.at[slot], adj_sem.at[slot]
        )

    def joint_copy(edge):
        low, high = max(edge * quarter - SIDE, 0), min(edge * quarter + SIDE, nx)
        return pltpu.make_async_copy(
            fwd_ref.at[:, pl.ds(low, high - low), :],
            ext.at[:, pl.ds(SIDE + low, high - low), pl.ds(LANES, ny)],
            joint_sem.at[edge],
        )

    def strip_copy(k):
        low = pl.multiple_of(peer(k) * quarter + SIDE, SIDE)
        rows = quarter - 2 * SIDE
        return pltpu.make_async_copy(
            fwd_ref.at[:, pl.ds(low, rows), :],
            ext.at[:, pl.ds(low + SIDE, rows), pl.ds(LANES, ny)],
            strip_sem.at[k],
        )

    for edge in range(bands + 1):
        joint_copy(edge).start()
    strip_copy(3).start()
    adj_copy(0).start()

    barrier = pltpu.get_barrier_semaphore()
    for k in range(1, bands):
        target = peer(k)
        pl.semaphore_signal(barrier, inc=1, device_id={"band": target})
    pl.semaphore_signal(barrier, inc=1, device_id={"gy": 1 - gy})

    @pl.when(gx > 0)
    def _():
        pl.semaphore_signal(barrier, inc=1, device_id={"gx": gx - 1})

    @pl.when(gx < gxs - 1)
    def _():
        pl.semaphore_signal(barrier, inc=1, device_id={"gx": gx + 1})

    below = (gx + gxs - 1) // gxs
    above = (2 * gxs - 2 - gx) // gxs
    pl.semaphore_wait(barrier, bands + below + above)

    def x_copy(up):
        source = nx - SIDE if up else 0
        target = 0 if up else SIDE + nx
        return pltpu.make_async_remote_copy(
            fwd_ref.at[:, pl.ds(source, SIDE), :],
            ext.at[:, pl.ds(target, SIDE), pl.ds(LANES, ny)],
            x_send.at[int(up)],
            x_recv.at[int(up)],
            device_id={"gx": gx + 1 if up else gx - 1},
        )

    def y_copy(t):
        rows = row_of(t)
        source = pl.multiple_of((1 - gy) * (ny - LANES), LANES)
        target = pl.multiple_of(gy * (LANES + ny), LANES)
        return pltpu.make_async_remote_copy(
            fwd_ref.at[:, pl.ds(rows, ROWS), pl.ds(source, LANES)],
            ext.at[:, pl.ds(rows + SIDE, ROWS), pl.ds(target, LANES)],
            y_send.at[t],
            y_recv.at[t],
            device_id={"gy": 1 - gy},
        )

    @pl.when(gx < gxs - 1)
    def _():
        x_copy(True).start()

    @pl.when(gx > 0)
    def _():
        x_copy(False).start()

    def start_y(t, carry):
        y_copy(t).start()
        return carry

    lax.fori_loop(0, pieces, start_y, 0)
    along_a[...] = band_matrix((ROWS, ROWS + 2 * SIDE), SIDE, False)
    along_b[...] = band_matrix((half + 2 * LANES, half), LANES, True)
    freq = jnp.full((1, ny), freq_ref[0], jnp.int32).astype(jnp.float32)
    span = jnp.full((1, ny), span_ref[0], jnp.int32).astype(jnp.float32)
    omega = (freq + 1.0) / FREQS
    beta = (span - (SPANS - 1) / 2.0) * 2.0 / SPANS
    weight = 1.0 / (0.5 + omega)
    coef[0:1] = weight / 12.0
    coef[1:2] = weight / 12.0
    coef[2:3] = -beta * weight
    coef[3:4] = omega * weight
    coef[4:5] = weight

    @pl.when(gx == 0)
    def _():
        ext[:, 0:SIDE, LANES:LANES + ny] = jnp.zeros((2 * comps, SIDE, ny), jnp.bfloat16)

    @pl.when(gx == gxs - 1)
    def _():
        ext[:, SIDE + nx:, LANES:LANES + ny] = jnp.zeros((2 * comps, SIDE, ny), jnp.bfloat16)

    @pl.when(gy == 0)
    def _():
        for p in range(2 * comps):
            ext[p, SIDE:SIDE + nx, 0:LANES] = jnp.zeros((nx, LANES), jnp.bfloat16)

    @pl.when(gy == 1)
    def _():
        for p in range(2 * comps):
            ext[p, SIDE:SIDE + nx, LANES + ny:] = jnp.zeros((nx, LANES), jnp.bfloat16)

    for edge in range(bands + 1):
        joint_copy(edge).wait()
    strip_copy(3).wait()
    for t in range(1, SLOTS):
        adj_copy(t).start()
    for k in (1, 2, 0):
        strip_copy(k).start()
    lax.fori_loop(pieces, steps, start_y, 0)

    @pl.when(gx > 0)
    def _():
        x_copy(True).wait_recv()

    @pl.when(gx < gxs - 1)
    def _():
        x_copy(False).wait_recv()

    def data_copy(phase, piece):
        return pltpu.make_async_remote_copy(
            sent.at[phase, piece], got.at[phase, piece],
            d_send.at[phase, piece], d_recv.at[phase, piece],
            device_id={"band": peer(1 + piece % 2)},
        )

    def sum_copy(piece):
        return pltpu.make_async_remote_copy(
            sent_sum.at[piece], got_sum.at[piece],
            d_send.at[2, piece], d_recv.at[2, piece],
            device_id={"band": peer(2 - piece % 2)},
        )

    def scale_copy(phase, piece):
        odd = piece % 2
        third = phase // 2
        return pltpu.make_async_remote_copy(
            sent_scale.at[phase, piece], got_scale.at[phase, piece],
            s_send.at[phase, piece], s_recv.at[phase, piece],
            device_id={"band": peer((1 + odd) * (1 - third) + (2 - odd) * third)},
        )

    fields = (0, 1, 2, 2, 3)

    def coded(value):
        most = jnp.maximum(jnp.max(jnp.abs(value), axis=0, keepdims=True), 1e-30)
        level = jnp.round(value * (LEVELS / most))
        return level.astype(jnp.int32).astype(jnp.int16), most * (1.0 / LEVELS)

    def step(t, carry):
        phase, piece = t // pieces, t % pieces
        rows = row_of(t)
        slot = t % SLOTS

        @pl.when(t == pieces)
        def _():
            strip_copy(1).wait()
            strip_copy(2).wait()

        @pl.when(t == 3 * pieces)
        def _():
            strip_copy(0).wait()

        adj_copy(t).wait()
        y_copy(t).wait_recv()
        acc[...] = jnp.zeros_like(acc)

        def add_comp(comp, carry):
            for h in range(ny // half):
                cols = pl.ds(h * half, half)
                dx, dy, q, a = [], [], [], []
                for part in range(2):
                    plane = part * comps + comp
                    tall = ext[plane, pl.ds(rows, ROWS + 2 * SIDE), pl.ds(LANES + h * half, half)]
                    wide = ext[plane, pl.ds(rows + SIDE, ROWS), pl.ds(h * half, half + 2 * LANES)]
                    dx.append(jnp.dot(along_a[...], tall, preferred_element_type=jnp.float32))
                    dy.append(jnp.dot(wide, along_b[...], preferred_element_type=jnp.float32))
                    q.append(wide[:, LANES:LANES + half].astype(jnp.float32))
                    a.append(adj[slot, plane, :, cols].astype(jnp.float32))
                acc[0, :, cols] += a[0] * dx[0] + a[1] * dx[1]
                acc[1, :, cols] += a[0] * dy[0] + a[1] * dy[1]
                acc[2, :, cols] += a[0] * q[1] - a[1] * q[0]
                acc[3, :, cols] += a[0] * q[0] + a[1] * q[1]
            return carry

        lax.fori_loop(0, comps, add_comp, 0)

        @pl.when(t + SLOTS < steps)
        def _():
            adj_copy(t + SLOTS).start()

        @pl.when(phase < 2)
        def _():
            for field in range(4):
                level, scale = coded(acc[field])
                sent[phase, piece, field] = level
                for out in range(5):
                    if fields[out] == field:
                        sent_scale[phase, piece, out:out + 1] = scale * coef[out:out + 1]
            data_copy(phase, piece).start()
            scale_copy(phase, piece).start()

        @pl.when(phase == 2)
        def _():
            data_copy(0, piece).wait_recv()
            scale_copy(0, piece).wait_recv()
            for out, field in enumerate(fields):
                other = got[0, piece, field].astype(jnp.int32).astype(jnp.float32)
                value = acc[field] * coef[out:out + 1] + other * got_scale[0, piece, out:out + 1]
                level, scale = coded(value)
                sent_sum[piece, out] = level
                sent_scale[2, piece, out:out + 1] = scale
            sum_copy(piece).start()
            scale_copy(2, piece).start()

        @pl.when(phase == 3)
        def _():
            for out, field in enumerate(fields):
                total[out, pl.ds(pl.multiple_of(piece * ROWS, ROWS), ROWS), :] = (
                    acc[field] * coef[out:out + 1]
                )

        return carry

    sent_scale[...] = jnp.zeros_like(sent_scale)
    lax.fori_loop(0, steps, step, 0)

    def out_copy(piece):
        rows = pl.ds(pl.multiple_of(piece * ROWS, ROWS), ROWS)
        return pltpu.make_async_copy(
            total.at[:, rows, :], out_ref.at[:, rows, :], out_sem.at[piece]
        )

    def add_one(piece, carry):
        data_copy(1, piece).wait_recv()
        scale_copy(1, piece).wait_recv()
        rows = pl.ds(pl.multiple_of(piece * ROWS, ROWS), ROWS)
        for out, field in enumerate(fields):
            value = got[1, piece, field].astype(jnp.int32).astype(jnp.float32)
            total[out, rows, :] += value * got_scale[1, piece, out:out + 1]
        return carry

    lax.fori_loop(0, pieces, add_one, 0)

    def add_sum(piece, carry):
        sum_copy(piece).wait_recv()
        scale_copy(2, piece).wait_recv()
        rows = pl.ds(pl.multiple_of(piece * ROWS, ROWS), ROWS)
        for out in range(5):
            value = got_sum[piece, out].astype(jnp.int32).astype(jnp.float32)
            total[out, rows, :] += value * got_scale[2, piece, out:out + 1]
        out_copy(piece).start()
        return carry

    lax.fori_loop(0, pieces, add_sum, 0)

    def finish(piece, carry):
        for phase in range(2):
            data_copy(phase, piece).wait_send()
        sum_copy(piece).wait_send()
        for phase in range(3):
            scale_copy(phase, piece).wait_send()
        return carry

    lax.fori_loop(0, pieces, finish, 0)

    def finish_y(t, carry):
        y_copy(t).wait_send()
        return carry

    lax.fori_loop(0, steps, finish_y, 0)

    @pl.when(gx < gxs - 1)
    def _():
        x_copy(True).wait_send()

    @pl.when(gx > 0)
    def _():
        x_copy(False).wait_send()

    def finish_out(piece, carry):
        out_copy(piece).wait()
        return carry

    lax.fori_loop(0, pieces, finish_out, 0)


def local(bands, gxs, forward, adjoint, freq_index, span_index):
    comps, nx, ny = forward.shape[2:]
    pieces = nx // bands // ROWS
    steps = bands * pieces
    planes = 2 * comps
    anywhere = pl.BlockSpec(memory_space=pl.ANY)
    scalar = pl.BlockSpec(memory_space=pltpu.SMEM)
    dma = pltpu.SemaphoreType.DMA
    total = pl.pallas_call(
        functools.partial(kernel, bands, gxs, comps, pieces),
        out_shape=jax.ShapeDtypeStruct((5, nx // bands, ny), jnp.float32),
        in_specs=[scalar, scalar, anywhere, anywhere],
        out_specs=anywhere,
        scratch_shapes=[
            pltpu.VMEM((planes, nx + 2 * SIDE, ny + 2 * LANES), jnp.bfloat16),
            pltpu.VMEM((SLOTS, planes, ROWS, ny), jnp.bfloat16),
            pltpu.VMEM((4, ROWS, ny), jnp.float32),
            pltpu.VMEM((ROWS, ROWS + 2 * SIDE), jnp.bfloat16),
            pltpu.VMEM((256 + 2 * LANES, 256), jnp.bfloat16),
            pltpu.VMEM((2, pieces, 4, ROWS, ny), jnp.int16),
            pltpu.VMEM((pieces, 5, ROWS, ny), jnp.int16),
            pltpu.VMEM((3, pieces, 8, ny), jnp.float32),
            pltpu.VMEM((2, pieces, 4, ROWS, ny), jnp.int16),
            pltpu.VMEM((pieces, 5, ROWS, ny), jnp.int16),
            pltpu.VMEM((3, pieces, 8, ny), jnp.float32),
            pltpu.VMEM((5, nx // bands, ny), jnp.float32),
            pltpu.VMEM((8, ny), jnp.float32),
            dma((bands + 1,)), dma((bands,)), dma((SLOTS,)), dma((2,)), dma((2,)), dma((steps,)), dma((steps,)),
            dma((3, pieces)), dma((3, pieces)),
            dma((3, pieces)), dma((3, pieces)), dma((pieces,)),
        ],
        compiler_params=pltpu.CompilerParams(
            collective_id=0, has_side_effects=True, vmem_limit_bytes=60 * 1024 * 1024
        ),
        cost_estimate=pl.CostEstimate(
            flops=20 * planes * nx * ny, bytes_accessed=4 * planes * nx * ny, transcendentals=0
        ),
    )(
        freq_index, span_index,
        forward.reshape(planes, nx, ny), adjoint.reshape(planes, nx, ny),
    )
    return total * (1.0 / math.sqrt(comps * bands * forward.shape[0]))


def solution(mesh):
    in_specs = (
        P("band", None, None, "gx", "gy"),
        P("band", None, None, "gx", "gy"),
        P("band"),
        P("band"),
    )
    out_specs = P(None, ("gx", "band"), "gy")
    body = functools.partial(local, mesh.shape["band"], mesh.shape["gx"])
    return jax.shard_map(body, mesh=mesh, in_specs=in_specs, out_specs=out_specs, check_vma=False)
```
